256 devices in a mesh: ctx: 64 (over x, z, y_lo), tp: 4 (over y_hi, core).
Axes of the slice: x: 4, y: 4 (y_hi: 2, y_lo: 2; y = y_hi * 2 + y_lo), z: 8, core: 2. Of those that a mesh axis runs over, the one named last changes fastest.
Arguments:
- queries: bfloat16 [512, 16384], P('ctx', 'tp'), may hold values from -100 to 100
- span_keys: bfloat16 [512, 1024], P('ctx', 'tp'), may hold values from -8 to 8
- span_values: bfloat16 [512, 1024], P('ctx', 'tp'), may hold values from -6 to 6
- cache_keys: bfloat16 [32768, 1024], P('ctx', 'tp'), may hold values from -6 to 6
- cache_values: bfloat16 [32768, 1024], P('ctx', 'tp'), may hold values from -6 to 6
- lengths: int32 [64], P('ctx'), may hold values from 1 to 512, 24576 in all
- start_pos: int32 [1], replicated, may hold values from 12288 to 24576
- w_out: bfloat16 [16384, 16384], P('tp', 'ctx'), may hold values from -3 to 3
Outputs:
- mixed: bfloat16 [512, 16384], P('tp', 'ctx')
The draws below stay inside these ranges and needn't reach their ends.
Inputs may be any that keep to these rules, and one draw needn't show every extreme that they name: All lengths together sum to 24576.
All inputs are finite; a program needn't handle non-finite values. No bound on the sum of `lengths` on one device may be relied on, other than what follows from the above.
Results may differ from the reference program's by a relative error of at most 0.007.
Values may be sent and summed in bfloat16 or wider, within the bound.
No kernel may reach another device: no remote copies, remote signals or barrier semaphores. Data moves between devices by JAX's collectives and lax.ppermute only.
A program may use at most 128 MiB of HBM per device.

```python
import math
import jax
import jax.numpy as jnp
import numpy as np
from jax import lax

D = 16384
HEADS = 128
KV_HEADS = 8
HEAD_DIM = 128
CACHE_DEV = 512
TOKENS = 512
CACHE_ROWS = 32768
TOTAL_VALID = 24576
N_CTX = 64


def draw_queries(key, part):
    key = jax.random.fold_in(key, 1)
    array_shape = (TOKENS, HEADS * HEAD_DIM)
    sample = jnp.clip(jax.random.normal(key, array_shape, jnp.float32), -6.0, 6.0)
    return sample.astype(jnp.bfloat16)


def draw_span_keys(key, part):
    key = jax.random.fold_in(key, 2)
    array_shape = (TOKENS, KV_HEADS * HEAD_DIM)
    sample = jnp.clip(jax.random.normal(key, array_shape, jnp.float32), -6.0, 6.0)
    return sample.astype(jnp.bfloat16)


def shard_levels(own_key, shape, split, low, largest):
    level, own = 1.0, jax.random.fold_in(own_key, 6)
    for axis_at, shards_of in split:
        heights = jnp.exp(jax.random.uniform(jax.random.fold_in(own, axis_at), (shards_of,), jnp.float32, low / len(split), largest / len(split)))
        level = level * jnp.repeat(heights, shape[axis_at] // shards_of).reshape([-1 if axis == axis_at else 1 for axis in range(len(shape))])
    return level


def profile(number_of, total, reach, lean):
    loads = [(1 << 20) // math.isqrt(grade ** lean) + 1 for grade in range(2, number_of + 1)]
    spare, holding = total - reach - (number_of - 1), [1] * (number_of - 1)
    while spare > 0:
        movable = [i for i in range(number_of - 1) if holding[i] < reach]
        whole, budget = sum([loads[i] for i in movable]), spare
        for i in movable:
            addition = min(reach - holding[i], max(1, budget * loads[i] // whole), spare)
            holding[i] = holding[i] + addition
            spare = spare - addition
    return np.array([reach] + holding)


def ragged_sizes(stream_key, number_of, total, bound, slope):
    if number_of == 2:
        one = jax.random.randint(stream_key, (), max(1, total - bound), min(bound, total - 1) + 1)
        return jnp.stack([one, total - one])
    sizes = jnp.asarray(profile(number_of, total, bound, slope), jnp.int32)
    couples = (number_of - 1) // 2
    giver, sink = sizes[1:1 + 2 * couples:2], sizes[2:2 + 2 * couples:2]
    slack = jnp.minimum(giver - 1, bound - sink)
    shifted = jax.random.randint(jax.random.fold_in(stream_key, 1), (couples,), 0, 1 << 20) % (slack + 1)
    sizes = sizes.at[1:1 + 2 * couples:2].set(giver - shifted).at[2:2 + 2 * couples:2].set(sink + shifted)
    return sizes[jax.random.permutation(jax.random.fold_in(stream_key, 2), number_of)]


def centred(key, dims, width, limit, shards=(), dtype=jnp.bfloat16):
    factor_of = shard_levels(key, dims, shards, -0.22, 0.18) if shards else 1.0
    drawn = jax.random.normal(key, dims, jnp.float32) * width * factor_of
    return jnp.minimum(jnp.maximum(drawn, -limit), limit).astype(dtype)


def setup_inputs(seed: int = 0) -> dict:
    key_of = jax.random.split(jax.random.key(seed), 9)
    return {
        "queries": draw_queries(jax.random.fold_in(key_of[8], 71), 0),
        "span_keys": draw_span_keys(jax.random.fold_in(key_of[8], 71), 0),
        "span_values": centred(key_of[2], (TOKENS, KV_HEADS * HEAD_DIM), 1.0, 6.0, ((0, 64), (1, 4))),
        "cache_keys": centred(key_of[3], (CACHE_ROWS, KV_HEADS * HEAD_DIM), 1.0, 6.0, ((0, 64), (1, 4))),
        "cache_values": centred(key_of[4], (CACHE_ROWS, KV_HEADS * HEAD_DIM), 1.0, 6.0, ((0, 64), (1, 4))),
        "lengths": ragged_sizes(key_of[5], N_CTX, TOTAL_VALID, CACHE_DEV, 2).astype(jnp.int32),
        "start_pos": jax.random.randint(key_of[6], (1,), TOTAL_VALID // 2, TOTAL_VALID + 1).astype(jnp.int32),
        "w_out": centred(key_of[7], (HEADS * HEAD_DIM, D), 0.5, 3.0, ((0, 4), (1, 64))),
    }


very_low = -1e+30

def partial_block(query_block, key_rows, value_rows, visible_mask):
    scores = jnp.einsum('rkge,cke->rkgc', query_block.astype(jnp.float32), key_rows.astype(jnp.float32))
    scores = scores * (1.0 / math.sqrt(HEAD_DIM))
    mask_full = visible_mask[:, None, None, :]
    masked = jnp.where(mask_full, scores, very_low)
    part_max = lax.optimization_barrier(jnp.max(masked, axis=-1))
    exp_terms = jnp.where(mask_full, jnp.exp(masked - part_max[..., None]), 0.0)
    part_sum = lax.optimization_barrier(jnp.sum(exp_terms, axis=-1))
    weights = lax.optimization_barrier(exp_terms.astype(jnp.bfloat16)).astype(jnp.float32)
    summed = jnp.einsum('rkgc,cke->rkge', weights, value_rows.astype(jnp.float32))
    part_out = (summed / jnp.maximum(part_sum, 1.0)[..., None]).astype(jnp.bfloat16)
    return (part_out, part_max, part_sum)

def absorb(running, part):
    top_score, numerator, denominator = running
    part_out, part_max, part_sum = part
    new_top = jnp.maximum(top_score, part_max)
    rescale = jnp.exp(top_score - new_top)
    share_now = part_sum * jnp.exp(part_max - new_top)
    numerator = numerator * rescale[..., None] + share_now[..., None] * part_out.astype(jnp.float32)
    denominator = denominator * rescale + share_now
    return (new_top, numerator, denominator)

def reference(queries, span_keys, span_values, cache_keys, cache_values, lengths, start_pos, w_out):
    group_size = HEADS // KV_HEADS
    own_queries = queries.reshape(TOKENS, KV_HEADS, group_size, HEAD_DIM)
    span_k = span_keys.reshape(TOKENS, KV_HEADS, HEAD_DIM)
    span_v = span_values.reshape(TOKENS, KV_HEADS, HEAD_DIM)
    offset = jnp.cumsum(lengths) - lengths
    visible_count = jnp.clip(start_pos[0] - offset, 0, lengths)
    positions = jnp.arange(TOKENS)
    causal = positions[None, :] <= positions[:, None]
    running = (jnp.full((TOKENS, KV_HEADS, group_size), very_low, jnp.float32), jnp.zeros((TOKENS, KV_HEADS, group_size, HEAD_DIM), jnp.float32), jnp.zeros((TOKENS, KV_HEADS, group_size), jnp.float32))
    running = absorb(running, partial_block(own_queries, span_k, span_v, causal))
    keys_by = cache_keys.reshape(N_CTX, CACHE_DEV, KV_HEADS, HEAD_DIM)
    values_by = cache_values.reshape(N_CTX, CACHE_DEV, KV_HEADS, HEAD_DIM)
    row_ids = jnp.arange(CACHE_DEV)

    def scan_step(carried, shard_item):
        key_rows, value_rows, shard_limit = shard_item
        visible_mask = (row_ids < shard_limit)[None, :]
        return (absorb(carried, partial_block(own_queries, key_rows, value_rows, visible_mask)), None)
    running, _ = lax.scan(scan_step, running, (keys_by, values_by, visible_count))
    top_score, numerator, denominator = running
    attention = (numerator / denominator[..., None]).astype(jnp.bfloat16).reshape(TOKENS, HEADS * HEAD_DIM)
    return jnp.dot(attention, w_out, preferred_element_type=jnp.float32).astype(jnp.bfloat16)
```

```python
import functools
import math

import jax
import jax.numpy as jnp
from jax import lax
from jax.experimental import pallas as pl
from jax.experimental.pallas import tpu as pltpu
from jax.sharding import Mesh, PartitionSpec as P

HEADS = 128
KV_HEADS = 8
HEAD_DIM = 128
GROUP = HEADS // KV_HEADS
HIDE = -1e30
SCALE = 1.0 / math.sqrt(HEAD_DIM)
LOG2E = 1.4426950408889634

X, Z, YL, YH, CORE = 4, 8, 2, 2, 2
ZY = Z * YL
CTX_AXES = ("x", "z", "yl")
TP_AXES = ("yh", "c")
ZY_AXES = ("z", "yl")
TOK = 8
ROWS = 512
SPAN = 16
GTOK = ZY * TOK
KV_LOCAL = 2
HEADS_LOCAL = KV_LOCAL * GROUP
WIDTH = HEADS_LOCAL * HEAD_DIM
CACHE = X * ROWS
COLS = CACHE + 128


def attend_kernel(info, q_ref, kv0, kv1, kv2, kv3, out_ref, keys, values, seen):
    lane = lax.broadcasted_iota(jnp.int32, (ROWS, 128), 1)
    row = lax.broadcasted_iota(jnp.int32, (ROWS, 128), 0)
    for k, kv in enumerate((kv0, kv1, kv2, kv3)):
        bias = jnp.where((lane == 0) & (row >= info[k]), HIDE, 0.0).astype(jnp.bfloat16)
        for g in range(KV_LOCAL):
            at = pl.ds(k * ROWS, ROWS)
            keys[g, at, 0:128] = kv[0:ROWS, g * 128 : (g + 1) * 128]
            keys[g, at, 128:256] = bias
            values[g, at, 0:128] = kv[0:ROWS, 256 + g * 128 : 256 + (g + 1) * 128]
            at = pl.ds(CACHE + k * SPAN, SPAN)
            keys[g, at, 0:128] = kv[ROWS : ROWS + SPAN, g * 128 : (g + 1) * 128]
            values[g, at, 0:128] = kv[ROWS : ROWS + SPAN, 256 + g * 128 : 256 + (g + 1) * 128]
    lane = lax.broadcasted_iota(jnp.int32, (128, 128), 1)
    row = lax.broadcasted_iota(jnp.int32, (128, 128), 0)
    marks = jnp.where((row < 64) & (lane == 64 + row), 1.0, 0.0) + jnp.where(
        (row >= 64) & (lane == 0), HIDE, 0.0
    )
    marks = marks.astype(jnp.bfloat16)
    for g in range(KV_LOCAL):
        keys[g, pl.ds(CACHE, 128), 128:256] = marks
        keys[g, pl.ds(CACHE + 64, 64), 0:128] = jnp.zeros((64, 128), jnp.bfloat16)
        values[g, pl.ds(CACHE + 64, 64), 0:128] = jnp.zeros((64, 128), jnp.bfloat16)
        values[g, :, 128:256] = jnp.ones((COLS, 128), jnp.bfloat16)
    slot = lane - 64
    part, inner = slot // SPAN, slot % SPAN
    first = jnp.where(
        part == 0, info[4], jnp.where(part == 1, info[5], jnp.where(part == 2, info[6], info[7]))
    )
    hidden = (inner >= TOK) | (first + inner > info[8] + row)
    extra = jnp.where(lane == 0, 1.0, jnp.where((slot >= 0) & hidden, HIDE, 0.0))
    seen[...] = extra.astype(jnp.bfloat16)

    def one_group(g):
        def body(step, stats):
            for j in range(4):
                h = g * GROUP + step * 4 + j
                at = pl.ds(pl.multiple_of(h * 128, 128), 128)
                query = jnp.concatenate([q_ref[:, at], seen[...]], axis=1)
                scores = lax.dot_general(
                    query, keys[g], (((1,), (1,)), ((), ())), preferred_element_type=jnp.float32
                )
                top = jnp.max(scores, axis=1, keepdims=True)
                weights = jnp.exp2((scores - top) * (SCALE * LOG2E)).astype(jnp.bfloat16)
                both = jnp.dot(weights, values[g], preferred_element_type=jnp.float32)
                total = both[:, 128:256]
                out_ref[:, at] = (both[:, 0:128] / total).astype(jnp.bfloat16)
                stats = jnp.where(lane % HEADS_LOCAL == h, top * SCALE + jnp.log(total), stats)
            return stats

        return body

    stats = jnp.zeros((GTOK, 128), jnp.float32)
    for g in range(KV_LOCAL):
        stats = lax.fori_loop(0, GROUP // 4, one_group(g), stats)
    high = stats.astype(jnp.bfloat16).astype(jnp.float32)
    rest = stats - high
    middle = rest.astype(jnp.bfloat16).astype(jnp.float32)
    low = rest - middle
    pieces = jnp.where(lane < 32, high, jnp.where(lane < 64, middle, low))
    out_ref[:, WIDTH : WIDTH + 128] = pieces.astype(jnp.bfloat16)


def attend(info, queries, parts):
    vmem = pl.BlockSpec(memory_space=pltpu.VMEM)
    return pl.pallas_call(
        attend_kernel,
        out_shape=jax.ShapeDtypeStruct((GTOK, WIDTH + 128), jnp.bfloat16),
        in_specs=[pl.BlockSpec(memory_space=pltpu.SMEM)] + [vmem] * 5,
        out_specs=vmem,
        scratch_shapes=[
            pltpu.VMEM((KV_LOCAL, COLS, 256), jnp.bfloat16),
            pltpu.VMEM((KV_LOCAL, COLS, 256), jnp.bfloat16),
            pltpu.VMEM((GTOK, 128), jnp.bfloat16),
        ],
        compiler_params=pltpu.CompilerParams(vmem_limit_bytes=32 << 20),
        cost_estimate=pl.CostEstimate(
            flops=8 * HEADS_LOCAL * GTOK * COLS * 128,
            bytes_accessed=4 << 20,
            transcendentals=HEADS_LOCAL * GTOK * COLS,
        ),
        name="attend",
    )(info, queries, *parts)


def merge_kernel(got, out_ref):
    pieces = got[:, :, WIDTH : WIDTH + 128].astype(jnp.float32)
    lse = pieces + (pltpu.roll(pieces, 96, 2) + pltpu.roll(pieces, 64, 2))
    share = jnp.exp(lse - jnp.max(lse, axis=0, keepdims=True))
    share = share / jnp.sum(share, axis=0, keepdims=True)
    for h in range(HEADS_LOCAL):
        at = slice(h * 128, (h + 1) * 128)
        merged = jnp.sum(share[:, :, h : h + 1] * got[:, :, at].astype(jnp.float32), axis=0)
        out_ref[:, :, at] = jnp.broadcast_to(merged.astype(jnp.bfloat16)[None], (ZY, TOK, 128))


def merge(got):
    vmem = pl.BlockSpec(memory_space=pltpu.VMEM)
    return pl.pallas_call(
        merge_kernel,
        out_shape=jax.ShapeDtypeStruct((ZY, TOK, WIDTH), jnp.bfloat16),
        in_specs=[vmem],
        out_specs=vmem,
        compiler_params=pltpu.CompilerParams(vmem_limit_bytes=16 << 20),
        cost_estimate=pl.CostEstimate(flops=2 << 20, bytes_accessed=2 << 20, transcendentals=4096),
        name="merge",
    )(got)


def along_x(v, k):
    return lax.ppermute(v, "x", [((i + k) % X, i) for i in range(X)])


def shards(queries, span_keys, span_values, cache_keys, cache_values, lengths, start_pos, w_out):
    x, zy = lax.axis_index("x"), lax.axis_index(ZY_AXES)
    tp = lax.axis_index(TP_AXES)
    spread = jnp.broadcast_to(queries[None], (ZY, TOK, WIDTH))
    gathered = lax.all_to_all(spread, ZY_AXES, 0, 0, tiled=True).reshape(GTOK, WIDTH)
    own = jnp.concatenate(
        [
            jnp.concatenate([cache_keys, span_keys, jnp.zeros_like(span_keys)], axis=0),
            jnp.concatenate([cache_values, span_values, jnp.zeros_like(span_values)], axis=0),
        ],
        axis=1,
    )
    parts = [own] + [along_x(own, k) for k in (1, 3, 2)]
    order = jnp.array([0, 1, 3, 2], jnp.int32)
    sizes = lax.all_to_all(
        jnp.broadcast_to(lengths[None], (X * ZY, 1)), CTX_AXES, 0, 0, tiled=True
    ).reshape(1, X * ZY)
    shard = ((x + order) % X) * ZY + zy
    index = jnp.arange(X * ZY, dtype=jnp.int32)[None]
    offset = jnp.sum(jnp.where(index < shard[:, None], sizes, 0), axis=1)
    filled = jnp.sum(jnp.where(index == shard[:, None], sizes, 0), axis=1)
    limit = jnp.clip(start_pos - offset, 0, filled)
    info = jnp.concatenate([limit, shard * TOK, (x * GTOK)[None]]).astype(jnp.int32)

    partial = attend(info, gathered, parts)

    w_held, _ = lax.optimization_barrier((w_out, parts[3]))
    weights = [w_out, along_x(w_held, 1), along_x(w_held, 2), along_x(w_held, 3)]

    got = lax.all_to_all(partial.reshape(ZY, TOK, WIDTH + 128), ZY_AXES, 0, 0, tiled=True)
    merged = lax.all_to_all(merge(got), ZY_AXES, 0, 0, tiled=True).reshape(GTOK, WIDTH)

    projected = jnp.stack(
        [
            jnp.dot(merged, w, preferred_element_type=jnp.float32).astype(jnp.bfloat16)
            for w in weights
        ]
    )
    total = None
    for r in range(X):
        block = lax.dynamic_index_in_dim(projected, (tp + r - x) % X, 0, keepdims=False)
        pairs = [(a * 4 + b, ((b + r) % X) * 4 + a) for a in range(X) for b in range(4)]
        term = lax.ppermute(block, ("x", "yh", "c"), pairs).astype(jnp.float32)
        total = term if total is None else total + term
    return total.astype(jnp.bfloat16)


def solution(mesh):
    fine = Mesh(mesh.devices.reshape(X, Z, YL, YH, CORE), CTX_AXES + TP_AXES)
    split = P(CTX_AXES, TP_AXES)
    return jax.shard_map(
        shards,
        mesh=fine,
        in_specs=(split, split, split, split, split, P(CTX_AXES), P(), P(TP_AXES, CTX_AXES)),
        out_specs=P(TP_AXES, CTX_AXES),
        check_vma=False,
    )
```

```python
import math

import jax
import jax.numpy as jnp
from jax import lax
from jax.experimental import pallas as pl
from jax.experimental.pallas import tpu as pltpu
from jax.sharding import Mesh, PartitionSpec as P

HEADS = 128
KV_HEADS = 8
HEAD_DIM = 128
GROUP = HEADS // KV_HEADS
HIDE = -1e30
SCALE = 1.0 / math.sqrt(HEAD_DIM)
LOG2E = 1.4426950408889634

X, ZQ, ZP, YL, YH, CORE = 4, 4, 2, 2, 2, 2
MEMBERS = 16
CTX_AXES = ("x", "zq", "zp", "yl")
TP_AXES = ("yh", "c")
NEAR_AXES = ("x", "zp", "yl")
COLUMN_AXES = ("zq", "zp", "yl")
TOK = 8
ROWS = 512
SPAN = 16
GTOK = MEMBERS * TOK
KV_LOCAL = 2
HEADS_LOCAL = KV_LOCAL * GROUP
WIDTH = HEADS_LOCAL * HEAD_DIM
PARTS = ZQ
CACHE = PARTS * ROWS
COLS = CACHE + 128
STEPS = (0, 1, 3, 2)


def step_of(k):
    return jnp.where(k == 2, 3, jnp.where(k == 3, 2, k))


def pack_kernel(queries, size0, size1, size2, size3, out_ref):
    lane = lax.broadcasted_iota(jnp.int32, (TOK, 128), 1)
    tail = jnp.zeros((TOK, 128), jnp.float32)
    for k, size in enumerate((size0, size1, size2, size3)):
        high = size[0] // 256
        low = size[0] - high * 256
        tail = jnp.where(lane == k, high.astype(jnp.float32), tail)
        tail = jnp.where(lane == PARTS + k, low.astype(jnp.float32), tail)
    out_ref[:, :, 0:WIDTH] = jnp.broadcast_to(queries[...][None], (MEMBERS, TOK, WIDTH))
    out_ref[:, :, WIDTH : WIDTH + 128] = jnp.broadcast_to(
        tail.astype(jnp.bfloat16)[None], (MEMBERS, TOK, 128)
    )


def pack(queries, sizes):
    vmem = pl.BlockSpec(memory_space=pltpu.VMEM)
    smem = pl.BlockSpec(memory_space=pltpu.SMEM)
    return pl.pallas_call(
        pack_kernel,
        out_shape=jax.ShapeDtypeStruct((MEMBERS, TOK, WIDTH + 128), jnp.bfloat16),
        in_specs=[vmem] + [smem] * PARTS,
        out_specs=vmem,
        compiler_params=pltpu.CompilerParams(vmem_limit_bytes=16 << 20),
        cost_estimate=pl.CostEstimate(flops=1 << 19, bytes_accessed=1 << 20, transcendentals=0),
        name="pack",
    )(queries, *sizes)


def visible_rows(info, tail):
    lane = lax.broadcasted_iota(jnp.int32, (GTOK, 128), 1)
    row = lax.broadcasted_iota(jnp.int32, (GTOK, 128), 0)
    source = row // TOK
    held = (row % TOK == 0) & (lane < 2 * PARTS)
    size = jnp.where(held, tail * jnp.where(lane < PARTS, 256.0, 1.0), 0.0)
    place = (info[2] + step_of(lane % PARTS)) % ZQ
    shard = (source // 4) * 16 + place * 4 + source % 4
    start = info[0].astype(jnp.float32)
    out = []
    for k in range(PARTS):
        own = info[1] * 16 + ((info[2] + STEPS[k]) % ZQ) * 4 + info[3]
        offset = jnp.sum(jnp.where(shard < own, size, 0.0), keepdims=True)
        filled = jnp.sum(jnp.where(shard == own, size, 0.0), keepdims=True)
        out.append(jnp.clip(start - offset, 0.0, filled))
    return out


def attend_kernel(info, q_ref, *refs):
    kvs, (out_ref, keys, values, seen) = refs[: 2 * PARTS], refs[2 * PARTS :]
    limits = visible_rows(info, q_ref[:, WIDTH : WIDTH + 128].astype(jnp.float32))
    lane = lax.broadcasted_iota(jnp.int32, (ROWS, 128), 1)
    row = lax.broadcasted_iota(jnp.int32, (ROWS, 128), 0).astype(jnp.float32)
    for k in range(PARTS):
        bias = jnp.where((lane == 0) & (row >= limits[k]), HIDE, 0.0).astype(jnp.bfloat16)
        for g in range(KV_LOCAL):
            kv = kvs[g * PARTS + k]
            at = pl.ds(k * ROWS, ROWS)
            keys[g, at, 0:128] = kv[0:ROWS, 0:128]
            keys[g, at, 128:256] = bias
            values[g, at, 0:128] = kv[0:ROWS, 128:256]
            at = pl.ds(CACHE + k * SPAN, SPAN)
            keys[g, at, 0:128] = kv[ROWS : ROWS + SPAN, 0:128]
            values[g, at, 0:128] = kv[ROWS : ROWS + SPAN, 128:256]
    lane = lax.broadcasted_iota(jnp.int32, (128, 128), 1)
    row = lax.broadcasted_iota(jnp.int32, (128, 128), 0)
    marks = jnp.where((row < 64) & (lane == 64 + row), 1.0, 0.0) + jnp.where(
        (row >= 64) & (lane == 0), HIDE, 0.0
    )
    for g in range(KV_LOCAL):
        keys[g, pl.ds(CACHE, 128), 128:256] = marks.astype(jnp.bfloat16)
        keys[g, pl.ds(CACHE + 64, 64), 0:128] = jnp.zeros((64, 128), jnp.bfloat16)
        values[g, pl.ds(CACHE + 64, 64), 0:128] = jnp.zeros((64, 128), jnp.bfloat16)
        values[g, :, 128:256] = jnp.ones((COLS, 128), jnp.bfloat16)
    slot = lane - 64
    part, inner = slot // SPAN, slot % SPAN
    shard = info[1] * 16 + ((info[2] + step_of(part)) % ZQ) * 4 + info[3]
    source = row // TOK
    chunk = (source // 4) * 16 + info[2] * 4 + source % 4
    hidden = (inner >= TOK) | (shard * TOK + inner > chunk * TOK + row % TOK)
    extra = jnp.where(lane == 0, 1.0, jnp.where((slot >= 0) & hidden, HIDE, 0.0))
    seen[...] = extra.astype(jnp.bfloat16)

    per = 2
    mask = jnp.concatenate([seen[...]] * per, axis=0)

    def one_group(g, stats):
        def columns(h):
            return pl.ds(pl.multiple_of((g * GROUP + h) * 128, 128), 128)

        def score(i):
            heads = [q_ref[:, columns(i * per + j)] for j in range(per)]
            query = jnp.concatenate([jnp.concatenate(heads, axis=0), mask], axis=1)
            return lax.dot_general(
                query, keys[g], (((1,), (1,)), ((), ())), preferred_element_type=jnp.float32
            )

        scores = score(0)
        for i in range(GROUP // per):
            later = score(i + 1) if i + 1 < GROUP // per else None
            top = jnp.max(scores, axis=1, keepdims=True)
            weights = jnp.exp2((scores - top) * (SCALE * LOG2E)).astype(jnp.bfloat16)
            both = jnp.dot(weights, values[g], preferred_element_type=jnp.float32)
            total = both[:, 128:256]
            outs = (both[:, 0:128] / total).astype(jnp.bfloat16)
            lse = top * SCALE + jnp.log(total)
            for j in range(per):
                h = i * per + j
                out_ref[:, columns(h)] = outs[j * GTOK : (j + 1) * GTOK]
                mine = lane % HEADS_LOCAL == g * GROUP + h
                stats = jnp.where(mine, lse[j * GTOK : (j + 1) * GTOK], stats)
            scores = later
        return stats

    stats = lax.fori_loop(0, KV_LOCAL, one_group, jnp.zeros((GTOK, 128), jnp.float32))
    high = stats.astype(jnp.bfloat16).astype(jnp.float32)
    rest = stats - high
    middle = rest.astype(jnp.bfloat16).astype(jnp.float32)
    low = rest - middle
    pieces = jnp.where(lane < HEADS_LOCAL, high, jnp.where(lane < 2 * HEADS_LOCAL, middle, low))
    out_ref[:, WIDTH : WIDTH + 128] = pieces.astype(jnp.bfloat16)


def attend(info, queries, parts):
    vmem = pl.BlockSpec(memory_space=pltpu.VMEM)
    return pl.pallas_call(
        attend_kernel,
        out_shape=jax.ShapeDtypeStruct((GTOK, WIDTH + 128), jnp.bfloat16),
        in_specs=[pl.BlockSpec(memory_space=pltpu.SMEM)] + [vmem] * (1 + 2 * PARTS),
        out_specs=vmem,
        scratch_shapes=[
            pltpu.VMEM((KV_LOCAL, COLS, 256), jnp.bfloat16),
            pltpu.VMEM((KV_LOCAL, COLS, 256), jnp.bfloat16),
            pltpu.VMEM((GTOK, 128), jnp.bfloat16),
        ],
        compiler_params=pltpu.CompilerParams(vmem_limit_bytes=32 << 20),
        cost_estimate=pl.CostEstimate(
            flops=8 * HEADS_LOCAL * GTOK * COLS * 128,
            bytes_accessed=4 << 20,
            transcendentals=HEADS_LOCAL * GTOK * COLS,
        ),
        name="attend",
    )(info, queries, *parts)


def merge_kernel(got, out_ref):
    pieces = got[:, :, WIDTH : WIDTH + 128].astype(jnp.float32)
    lse = pieces + (pltpu.roll(pieces, 96, 2) + pltpu.roll(pieces, 64, 2))
    share = jnp.exp(lse - jnp.max(lse, axis=0, keepdims=True))
    share = share / jnp.sum(share, axis=0, keepdims=True)
    for h in range(HEADS_LOCAL):
        at = slice(h * 128, (h + 1) * 128)
        merged = jnp.sum(share[:, :, h : h + 1] * got[:, :, at].astype(jnp.float32), axis=0)
        out_ref[:, :, at] = jnp.broadcast_to(merged.astype(jnp.bfloat16)[None], (MEMBERS, TOK, 128))


def merge(got):
    vmem = pl.BlockSpec(memory_space=pltpu.VMEM)
    return pl.pallas_call(
        merge_kernel,
        out_shape=jax.ShapeDtypeStruct((MEMBERS, TOK, WIDTH), jnp.bfloat16),
        in_specs=[vmem],
        out_specs=vmem,
        compiler_params=pltpu.CompilerParams(vmem_limit_bytes=16 << 20),
        cost_estimate=pl.CostEstimate(flops=2 << 20, bytes_accessed=2 << 20, transcendentals=4096),
        name="merge",
    )(got)


def along(v, axis, k):
    return lax.ppermute(v, axis, [((i + k) % 4, i) for i in range(4)])


def after(v, *earlier):
    return lax.optimization_barrier((v, *earlier))[0]


def shards(queries, span_keys, span_values, cache_keys, cache_values, lengths, start_pos, w_out):
    x, zq, near = lax.axis_index("x"), lax.axis_index("zq"), lax.axis_index(("zp", "yl"))
    tp = lax.axis_index(TP_AXES)
    info = jnp.stack([start_pos[0], x, zq, near]).astype(jnp.int32)

    own = []
    for g in range(KV_LOCAL):
        at = slice(g * 128, (g + 1) * 128)
        empty = jnp.zeros((TOK, 128), jnp.bfloat16)
        own.append(
            jnp.concatenate(
                [
                    jnp.concatenate([cache_keys[:, at], span_keys[:, at], empty], axis=0),
                    jnp.concatenate([cache_values[:, at], span_values[:, at], empty], axis=0),
                ],
                axis=1,
            )
        )
    following = [along(v, "zq", 1) for v in own]
    previous = [along(v, "zq", 3) for v in own]
    far = [along(following[0], "zq", 1), along(previous[1], "zq", 3)]
    parts = [v for g in range(KV_LOCAL) for v in (own[g], following[g], previous[g], far[g])]

    sizes = [lengths] + [along(lengths, "zq", k) for k in STEPS[1:]]
    packed = pack(queries, sizes)
    gathered = lax.all_to_all(packed, NEAR_AXES, 0, 0, tiled=True).reshape(GTOK, WIDTH + 128)

    wide = w_out.shape[0] // 2
    own_w = [w_out[:wide], w_out[wide:]]
    held = after(own_w[0], following[1], previous[1])
    next_a, last_a = along(held, "x", 1), along(held, "x", 3)
    held = after(own_w[1], next_a, last_a)
    next_b, last_b = along(held, "x", 1), along(held, "x", 3)
    far_a = along(after(next_a, next_b, last_b), "x", 1)
    far_b = along(after(last_b, next_b), "x", 3)
    weights = [(own_w[0], own_w[1]), (next_a, next_b), (far_a, far_b), (last_a, last_b)]

    partial = attend(info, gathered, parts)
    partial = after(partial, next_a, last_a)
    got = lax.all_to_all(
        partial.reshape(MEMBERS, TOK, WIDTH + 128), NEAR_AXES, 0, 0, tiled=True
    )
    copies = after(merge(got), next_b, last_b)
    merged = lax.all_to_all(copies, COLUMN_AXES, 0, 0, tiled=True).reshape(GTOK, WIDTH)

    projected = jnp.stack(
        [
            (
                jnp.dot(merged[:, :wide], a, preferred_element_type=jnp.float32)
                + jnp.dot(merged[:, wide:], b, preferred_element_type=jnp.float32)
            ).astype(jnp.bfloat16)
            for a, b in weights
        ]
    )
    total = None
    for r in range(X):
        block = lax.dynamic_index_in_dim(projected, (tp + r - x) % X, 0, keepdims=False)
        pairs = [(a * 4 + b, ((b + r) % X) * 4 + a) for a in range(X) for b in range(4)]
        term = lax.ppermute(block, ("x", "yh", "c"), pairs).astype(jnp.float32)
        total = term if total is None else total + term
    return total.astype(jnp.bfloat16)


def solution(mesh):
    fine = Mesh(mesh.devices.reshape(X, ZQ, ZP, YL, YH, CORE), CTX_AXES + TP_AXES)
    split = P(CTX_AXES, TP_AXES)
    return jax.shard_map(
        shards,
        mesh=fine,
        in_specs=(split, split, split, split, split, P(CTX_AXES), P(), P(TP_AXES, CTX_AXES)),
        out_specs=P(TP_AXES, CTX_AXES),
        check_vma=False,
    )
```

```python
import math

import jax
import jax.numpy as jnp
from jax import lax
from jax.experimental import pallas as pl
from jax.experimental.pallas import tpu as pltpu
from jax.sharding import Mesh, PartitionSpec as P

HEADS = 128
KV_HEADS = 8
HEAD_DIM = 128
GROUP = HEADS // KV_HEADS
HIDE = -1e30
SCALE = 1.0 / math.sqrt(HEAD_DIM)
LOG2E = 1.4426950408889634

X, Z, YL, YH, CORE = 4, 8, 2, 2, 2
MEMBERS = Z * YL
CTX_AXES = ("x", "z", "yl")
TP_AXES = ("yh", "c")
ZY_AXES = ("z", "yl")
TOK = 8
ROWS = 512
SPAN = 16
GTOK = MEMBERS * TOK
KV_LOCAL = 2
HEADS_LOCAL = KV_LOCAL * GROUP
WIDTH = HEADS_LOCAL * HEAD_DIM
PARTS = X
CACHE = PARTS * ROWS
COLS = CACHE + 128
STEPS = (0, 1, 3, 2)


def step_of(k):
    return jnp.where(k == 2, 3, jnp.where(k == 3, 2, k))


def collect_kernel(cache_k, cache_v, span_k, span_v, own, sems):
    copies = []
    for side, cache in enumerate((cache_k, cache_v)):
        for g in range(KV_LOCAL):
            copies.append(
                pltpu.make_async_copy(
                    cache.at[:, pl.ds(g * 128, 128)],
                    own.at[pl.ds(g * (ROWS + SPAN), ROWS), pl.ds(side * 128, 128)],
                    sems.at[side * KV_LOCAL + g],
                )
            )
    for copy in copies:
        copy.start()
    empty = jnp.zeros((TOK, 256), jnp.float32)
    for side, span in enumerate((span_k, span_v)):
        padded = jnp.concatenate([span[...].astype(jnp.float32), empty], axis=0)
        padded = padded.astype(jnp.bfloat16)
        for g in range(KV_LOCAL):
            at = g * (ROWS + SPAN) + ROWS
            own[at : at + SPAN, side * 128 : side * 128 + 128] = padded[:, g * 128 : g * 128 + 128]
    for copy in copies:
        copy.wait()


def collect(cache_keys, cache_values, span_keys, span_values):
    vmem, either = pl.BlockSpec(memory_space=pltpu.VMEM), pl.BlockSpec(memory_space=pl.ANY)
    return pl.pallas_call(
        collect_kernel,
        out_shape=jax.ShapeDtypeStruct((KV_LOCAL * (ROWS + SPAN), 256), jnp.bfloat16),
        in_specs=[either, either, vmem, vmem],
        out_specs=vmem,
        scratch_shapes=[pltpu.SemaphoreType.DMA((2 * KV_LOCAL,))],
        compiler_params=pltpu.CompilerParams(vmem_limit_bytes=4 << 20),
        cost_estimate=pl.CostEstimate(flops=1 << 16, bytes_accessed=1 << 20, transcendentals=0),
        name="collect",
    )(cache_keys, cache_values, span_keys, span_values)


def pack_kernel(queries, size0, size1, size2, size3, later, message):
    del later
    lane = lax.broadcasted_iota(jnp.int32, (TOK, 128), 1)
    tail = jnp.zeros((TOK, 128), jnp.int32)
    for k, size in enumerate((size0, size1, size2, size3)):
        high = size[0] // 256
        tail = jnp.where(lane == k, high, tail)
        tail = jnp.where(lane == PARTS + k, size[0] - high * 256, tail)
    tail = tail.astype(jnp.float32).astype(jnp.bfloat16)
    message[:, :, 0:WIDTH] = jnp.broadcast_to(queries[...][None], (MEMBERS, TOK, WIDTH))
    message[:, :, WIDTH : WIDTH + 128] = jnp.broadcast_to(tail[None], (MEMBERS, TOK, 128))


def pack(queries, sizes, own):
    vmem = pl.BlockSpec(memory_space=pltpu.VMEM)
    smem = pl.BlockSpec(memory_space=pltpu.SMEM)
    return pl.pallas_call(
        pack_kernel,
        out_shape=jax.ShapeDtypeStruct((MEMBERS, TOK, WIDTH + 128), jnp.bfloat16),
        in_specs=[vmem] + [smem] * PARTS + [pl.BlockSpec(memory_space=pl.ANY)],
        out_specs=vmem,
        compiler_params=pltpu.CompilerParams(vmem_limit_bytes=4 << 20),
        cost_estimate=pl.CostEstimate(flops=1 << 19, bytes_accessed=1 << 20, transcendentals=0),
        name="pack",
    )(queries, *sizes, own)


def visible_rows(info, tail):
    lane = lax.broadcasted_iota(jnp.int32, (GTOK, 128), 1)
    row = lax.broadcasted_iota(jnp.int32, (GTOK, 128), 0)
    held = (row % TOK == 0) & (lane < 2 * PARTS)
    size = jnp.where(held, tail * jnp.where(lane < PARTS, 256.0, 1.0), 0.0)
    shard = ((info[1] + step_of(lane % PARTS)) % X) * MEMBERS + row // TOK
    start = info[0].astype(jnp.float32)
    out = []
    for k in range(PARTS):
        own = ((info[1] + STEPS[k]) % X) * MEMBERS + info[2]
        offset = jnp.sum(jnp.where(shard < own, size, 0.0), keepdims=True)
        filled = jnp.sum(jnp.where(shard == own, size, 0.0), keepdims=True)
        out.append(jnp.clip(start - offset, 0.0, filled))
    return out


def attend_kernel(info, q_ref, own, after_, before, far0, far1, *refs):
    out_ref, keys, values, seen = refs
    limits = visible_rows(info, q_ref[:, WIDTH : WIDTH + 128].astype(jnp.float32))
    both = ROWS + SPAN
    kvs = [ref.at[pl.ds(g * both, both)] for g in range(KV_LOCAL) for ref in (own, after_, before)]
    kvs = kvs[:3] + [far0] + kvs[3:] + [far1]
    lane = lax.broadcasted_iota(jnp.int32, (ROWS, 128), 1)
    row = lax.broadcasted_iota(jnp.int32, (ROWS, 128), 0).astype(jnp.float32)
    for k in range(PARTS):
        bias = jnp.where((lane == 0) & (row >= limits[k]), HIDE, 0.0).astype(jnp.bfloat16)
        for g in range(KV_LOCAL):
            kv = kvs[g * PARTS + k]
            at = pl.ds(k * ROWS, ROWS)
            keys[g, at, 0:128] = kv[0:ROWS, 0:128]
            keys[g, at, 128:256] = bias
            values[g, at, 0:128] = kv[0:ROWS, 128:256]
            at = pl.ds(CACHE + k * SPAN, SPAN)
            keys[g, at, 0:128] = kv[ROWS : ROWS + SPAN, 0:128]
            values[g, at, 0:128] = kv[ROWS : ROWS + SPAN, 128:256]
    lane = lax.broadcasted_iota(jnp.int32, (128, 128), 1)
    row = lax.broadcasted_iota(jnp.int32, (128, 128), 0)
    marks = jnp.where((row < 64) & (lane == 64 + row), 1.0, 0.0) + jnp.where(
        (row >= 64) & (lane == 0), HIDE, 0.0
    )
    for g in range(KV_LOCAL):
        keys[g, pl.ds(CACHE, 128), 128:256] = marks.astype(jnp.bfloat16)
        keys[g, pl.ds(CACHE + 64, 64), 0:128] = jnp.zeros((64, 128), jnp.bfloat16)
        values[g, pl.ds(CACHE + 64, 64), 0:128] = jnp.zeros((64, 128), jnp.bfloat16)
        values[g, :, 128:256] = jnp.ones((COLS, 128), jnp.bfloat16)
    slot = lane - 64
    part, inner = slot // SPAN, slot % SPAN
    shard = ((info[1] + step_of(part)) % X) * MEMBERS + info[2]
    hidden = (inner >= TOK) | (shard * TOK + inner > info[1] * GTOK + row)
    extra = jnp.where(lane == 0, 1.0, jnp.where((slot >= 0) & hidden, HIDE, 0.0))
    seen[...] = extra.astype(jnp.bfloat16)

    per = 2
    mask = jnp.concatenate([seen[...]] * per, axis=0)

    def one_group(g, stats):
        def columns(h):
            return pl.ds(pl.multiple_of((g * GROUP + h) * 128, 128), 128)

        def score(i):
            heads = [q_ref[:, columns(i * per + j)] for j in range(per)]
            query = jnp.concatenate([jnp.concatenate(heads, axis=0), mask], axis=1)
            return lax.dot_general(
                query, keys[g], (((1,), (1,)), ((), ())), preferred_element_type=jnp.float32
            )

        scores = score(0)
        for i in range(GROUP // per):
            later = score(i + 1) if i + 1 < GROUP // per else None
            top = jnp.max(scores, axis=1, keepdims=True)
            weights = jnp.exp2((scores - top) * (SCALE * LOG2E)).astype(jnp.bfloat16)
            both = jnp.dot(weights, values[g], preferred_element_type=jnp.float32)
            total = both[:, 128:256]
            outs = (both[:, 0:128] / total).astype(jnp.bfloat16)
            lse = top * SCALE + jnp.log(total)
            for j in range(per):
                h = i * per + j
                out_ref[:, columns(h)] = outs[j * GTOK : (j + 1) * GTOK]
                mine = lane % HEADS_LOCAL == g * GROUP + h
                stats = jnp.where(mine, lse[j * GTOK : (j + 1) * GTOK], stats)
            scores = later
        return stats

    stats = lax.fori_loop(0, KV_LOCAL, one_group, jnp.zeros((GTOK, 128), jnp.float32))
    high = stats.astype(jnp.bfloat16).astype(jnp.float32)
    rest = stats - high
    middle = rest.astype(jnp.bfloat16).astype(jnp.float32)
    low = rest - middle
    pieces = jnp.where(lane < HEADS_LOCAL, high, jnp.where(lane < 2 * HEADS_LOCAL, middle, low))
    out_ref[:, WIDTH : WIDTH + 128] = pieces.astype(jnp.bfloat16)


def attend(info, queries, parts):
    vmem = pl.BlockSpec(memory_space=pltpu.VMEM)
    return pl.pallas_call(
        attend_kernel,
        out_shape=jax.ShapeDtypeStruct((GTOK, WIDTH + 128), jnp.bfloat16),
        in_specs=[pl.BlockSpec(memory_space=pltpu.SMEM)] + [vmem] * 6,
        out_specs=vmem,
        scratch_shapes=[
            pltpu.VMEM((KV_LOCAL, COLS, 256), jnp.bfloat16),
            pltpu.VMEM((KV_LOCAL, COLS, 256), jnp.bfloat16),
            pltpu.VMEM((GTOK, 128), jnp.bfloat16),
        ],
        compiler_params=pltpu.CompilerParams(vmem_limit_bytes=20 << 20),
        cost_estimate=pl.CostEstimate(
            flops=8 * HEADS_LOCAL * GTOK * COLS * 128,
            bytes_accessed=4 << 20,
            transcendentals=HEADS_LOCAL * GTOK * COLS,
        ),
        name="attend",
    )(info, queries, *parts)


def merge_kernel(got, out_ref):
    pieces = got[:, :, WIDTH : WIDTH + 128].astype(jnp.float32)
    lse = pieces + (pltpu.roll(pieces, 96, 2) + pltpu.roll(pieces, 64, 2))
    share = jnp.exp(lse - jnp.max(lse, axis=0, keepdims=True))
    share = share / jnp.sum(share, axis=0, keepdims=True)
    for h in range(HEADS_LOCAL):
        at = slice(h * 128, (h + 1) * 128)
        merged = jnp.sum(share[:, :, h : h + 1] * got[:, :, at].astype(jnp.float32), axis=0)
        out_ref[:, :, at] = jnp.broadcast_to(merged.astype(jnp.bfloat16)[None], (MEMBERS, TOK, 128))


def merge(got):
    vmem = pl.BlockSpec(memory_space=pltpu.VMEM)
    return pl.pallas_call(
        merge_kernel,
        out_shape=jax.ShapeDtypeStruct((MEMBERS, TOK, WIDTH), jnp.bfloat16),
        in_specs=[vmem],
        out_specs=vmem,
        compiler_params=pltpu.CompilerParams(vmem_limit_bytes=6 << 20),
        cost_estimate=pl.CostEstimate(flops=2 << 20, bytes_accessed=2 << 20, transcendentals=4096),
        name="merge",
    )(got)


def project_kernel(info, merged, *refs):
    pieces, out_ref = iter(refs[:-1]), refs[-1]
    for k in range(X):
        total, at = None, 0
        while at < WIDTH:
            w = next(pieces)
            rows = w.shape[0]
            term = jnp.dot(merged[:, at : at + rows], w[...], preferred_element_type=jnp.float32)
            total = term if total is None else total + term
            at += rows
        out_ref[(k + info[0] - info[1] + X) % X] = total.astype(jnp.bfloat16)


def project(info, merged, weights):
    vmem = pl.BlockSpec(memory_space=pltpu.VMEM)
    pieces = [w for part in weights for w in part]
    return pl.pallas_call(
        project_kernel,
        out_shape=jax.ShapeDtypeStruct((X, GTOK, 256), jnp.bfloat16),
        in_specs=[pl.BlockSpec(memory_space=pltpu.SMEM)] + [vmem] * (1 + len(pieces)),
        out_specs=vmem,
        compiler_params=pltpu.CompilerParams(vmem_limit_bytes=12 << 20),
        cost_estimate=pl.CostEstimate(
            flops=2 * GTOK * WIDTH * 256 * X, bytes_accessed=10 << 20, transcendentals=0
        ),
        name="project",
    )(info, merged, *pieces)


def along(v, axis, k):
    return lax.ppermute(v, axis, [((i + k) % 4, i) for i in range(4)])


def after(v, *earlier):
    return lax.optimization_barrier((v, *earlier))[0]


def shards(queries, span_keys, span_values, cache_keys, cache_values, lengths, start_pos, w_out):
    x, zy = lax.axis_index("x"), lax.axis_index(ZY_AXES)
    tp = lax.axis_index(TP_AXES)
    info = jnp.stack([start_pos[0], x, zy]).astype(jnp.int32)

    sizes = [lengths] + [along(lengths, "x", k) for k in STEPS[1:]]
    own = collect(cache_keys, cache_values, span_keys, span_values)
    following, previous = along(own, "x", 1), along(own, "x", 3)
    far0 = along(following[: ROWS + SPAN], "x", 1)
    far1 = along(previous[ROWS + SPAN :], "x", 3)

    packed = pack(queries, sizes, own)
    gathered = lax.all_to_all(packed, ZY_AXES, 0, 0, tiled=True).reshape(GTOK, WIDTH + 128)

    half = WIDTH // 2
    own_w = [w_out[:half], w_out[half:]]
    held = after(own_w[0], far0, far1)
    next0, last0 = along(held, "x", 1), along(held, "x", 3)
    held = after(own_w[1], next0, last0)
    next1, last1 = along(held, "x", 1), along(held, "x", 3)
    far_w0 = along(after(next0, next1, last1), "x", 1)
    far_w1 = along(after(last1, next1), "x", 3)
    weights = [own_w, [next0, next1], [far_w0, far_w1], [last0, last1]]

    partial = attend(info, gathered, [own, following, previous, far0, far1])
    partial = after(partial, next0, last0)
    got = lax.all_to_all(partial.reshape(MEMBERS, TOK, WIDTH + 128), ZY_AXES, 0, 0, tiled=True)
    copies = after(merge(got), next1, last1)
    merged = lax.all_to_all(copies, ZY_AXES, 0, 0, tiled=True).reshape(GTOK, WIDTH)

    projected = project(jnp.stack([x, tp]).astype(jnp.int32), merged, weights)
    total = None
    for r in range(X):
        pairs = [(a * 4 + b, ((b + r) % X) * 4 + a) for a in range(X) for b in range(4)]
        term = lax.ppermute(projected[r], ("x", "yh", "c"), pairs).astype(jnp.float32)
        total = term if total is None else total + term
    return total.astype(jnp.bfloat16)


def solution(mesh):
    fine = Mesh(mesh.devices.reshape(X, Z, YL, YH, CORE), CTX_AXES + TP_AXES)
    split = P(CTX_AXES, TP_AXES)
    return jax.shard_map(
        shards,
        mesh=fine,
        in_specs=(split, split, split, split, split, P(CTX_AXES), P(), P(TP_AXES, CTX_AXES)),
        out_specs=P(TP_AXES, CTX_AXES),
        check_vma=False,
    )
```

```python
import math

import jax
import jax.numpy as jnp
from jax import lax
from jax.experimental import pallas as pl
from jax.experimental.pallas import tpu as pltpu
from jax.sharding import Mesh, PartitionSpec as P

HEADS = 128
KV_HEADS = 8
HEAD_DIM = 128
GROUP = HEADS // KV_HEADS
HIDE = -1e30
SCALE = 1.0 / math.sqrt(HEAD_DIM)
LOG2E = 1.4426950408889634

X, ZQ, ZP, YL, YH, CORE = 4, 4, 2, 2, 2, 2
NEAR = ZP * YL
MEMBERS = ZQ * NEAR
CTX_AXES = ("x", "zq", "zp", "yl")
TP_AXES = ("yh", "c")
NEAR_AXES = ("zp", "yl")
ZY_AXES = ("zq", "zp", "yl")
TOK = 8
ROWS = 512
SPAN = 16
GTOK = MEMBERS * TOK
GATHERED = ZQ * TOK
KV_LOCAL = 2
HEADS_LOCAL = KV_LOCAL * GROUP
WIDTH = HEADS_LOCAL * HEAD_DIM
PARTS = X
STRIDE = ROWS + SPAN
COLS = 2176
STEPS = (0, 1, 3, 2)


def step_of(k):
    return jnp.where(k == 2, 3, jnp.where(k == 3, 2, k))


def collect_kernel(cache_k, cache_v, span_k, span_v, own, sems):
    copies = []
    for side, cache in enumerate((cache_k, cache_v)):
        for g in range(KV_LOCAL):
            copies.append(
                pltpu.make_async_copy(
                    cache.at[:, pl.ds(g * 128, 128)],
                    own.at[pl.ds(g * (ROWS + SPAN), ROWS), pl.ds(side * 128, 128)],
                    sems.at[side * KV_LOCAL + g],
                )
            )
    for copy in copies:
        copy.start()
    empty = jnp.zeros((TOK, 256), jnp.float32)
    for side, span in enumerate((span_k, span_v)):
        padded = jnp.concatenate([span[...].astype(jnp.float32), empty], axis=0)
        padded = padded.astype(jnp.bfloat16)
        for g in range(KV_LOCAL):
            at = g * (ROWS + SPAN) + ROWS
            own[at : at + SPAN, side * 128 : side * 128 + 128] = padded[:, g * 128 : g * 128 + 128]
    for copy in copies:
        copy.wait()


def collect(cache_keys, cache_values, span_keys, span_values):
    vmem, either = pl.BlockSpec(memory_space=pltpu.VMEM), pl.BlockSpec(memory_space=pl.ANY)
    return pl.pallas_call(
        collect_kernel,
        out_shape=pltpu.HBM((KV_LOCAL * (ROWS + SPAN), 256), jnp.bfloat16),
        in_specs=[either, either, vmem, vmem],
        out_specs=vmem,
        scratch_shapes=[pltpu.SemaphoreType.DMA((2 * KV_LOCAL,))],
        compiler_params=pltpu.CompilerParams(vmem_limit_bytes=4 << 20),
        cost_estimate=pl.CostEstimate(flops=1 << 16, bytes_accessed=1 << 20, transcendentals=0),
        name="collect",
    )(cache_keys, cache_values, span_keys, span_values)


def pack_kernel(queries, size0, size1, size2, size3, message):
    lane = lax.broadcasted_iota(jnp.int32, (TOK, 128), 1)
    tail = jnp.zeros((TOK, 128), jnp.int32)
    for k, size in enumerate((size0, size1, size2, size3)):
        high = size[0] // 256
        tail = jnp.where(lane == k, high, tail)
        tail = jnp.where(lane == PARTS + k, size[0] - high * 256, tail)
    message[:, 0:WIDTH] = queries[...]
    message[:, WIDTH : WIDTH + 128] = tail.astype(jnp.float32).astype(jnp.bfloat16)


def pack(queries, sizes):
    vmem = pl.BlockSpec(memory_space=pltpu.VMEM)
    return pl.pallas_call(
        pack_kernel,
        out_shape=jax.ShapeDtypeStruct((TOK, WIDTH + 128), jnp.bfloat16),
        in_specs=[vmem] + [pl.BlockSpec(memory_space=pltpu.SMEM)] * PARTS,
        out_specs=vmem,
        compiler_params=pltpu.CompilerParams(vmem_limit_bytes=2 << 20),
        cost_estimate=pl.CostEstimate(flops=1 << 16, bytes_accessed=1 << 17, transcendentals=0),
        name="pack",
    )(queries, *sizes)


def places(zq, near):
    return [((zq + b) % ZQ) * NEAR + (near + c) % NEAR for c in range(NEAR) for b in range(ZQ)]


def place_of(rows, zq, near):
    return ((zq + (rows // TOK) % ZQ) % ZQ) * NEAR + (near + rows // GATHERED) % NEAR


def visible_rows(info, tail):
    lane = lax.broadcasted_iota(jnp.int32, (GTOK, 128), 1)
    row = lax.broadcasted_iota(jnp.int32, (GTOK, 128), 0)
    held = (row % TOK == 0) & (lane < 2 * PARTS)
    size = jnp.where(held, tail * jnp.where(lane < PARTS, 256.0, 1.0), 0.0)
    x = (info[1] + step_of(lane % PARTS)) % X
    shard = x * MEMBERS + place_of(row, info[2], info[3])
    start = info[0].astype(jnp.float32)
    out = []
    for k in range(PARTS):
        own = ((info[1] + STEPS[k]) % X) * MEMBERS + info[2] * NEAR + info[3]
        offset = jnp.sum(jnp.where(shard < own, size, 0.0), keepdims=True)
        filled = jnp.sum(jnp.where(shard == own, size, 0.0), keepdims=True)
        out.append(jnp.clip(start - offset, 0.0, filled))
    return out


def attend_kernel(info, *refs):
    q_hbm, (own, following, previous, far0, far1) = refs[:NEAR], refs[NEAR : NEAR + 5]
    out_hbm, keys, values, seen, q_ref, res_ref, stat_ref, out_ref = refs[NEAR + 5 : NEAR + 13]
    kv_sems, q_sems, out_sems = refs[NEAR + 13 :]
    half = WIDTH // KV_LOCAL
    spans = [pl.ds(g * half, half) for g in range(KV_LOCAL)] + [pl.ds(WIDTH, 128)]

    def fetches(i):
        return [
            pltpu.make_async_copy(
                q_hbm[c].at[:, spans[i]],
                q_ref.at[pl.ds(c * GATHERED, GATHERED), spans[i]],
                q_sems.at[i * NEAR + c],
            )
            for c in range(NEAR)
        ]

    def loads(g):
        copies = []
        for k, kv in enumerate((own, following, previous, (far0, far1)[g])):
            first = 0 if k == PARTS - 1 else g * STRIDE
            for side, to in enumerate((keys, values)):
                copies.append(
                    pltpu.make_async_copy(
                        kv.at[pl.ds(first, STRIDE), pl.ds(side * 128, 128)],
                        to.at[g, pl.ds(k * STRIDE, STRIDE), pl.ds(0, 128)],
                        kv_sems.at[(g * PARTS + k) * 2 + side],
                    )
                )
        return copies

    def store(i):
        return pltpu.make_async_copy(
            out_ref.at[:, spans[i]], out_hbm.at[:, spans[i]], out_sems.at[i]
        )

    for copy in fetches(KV_LOCAL):
        copy.start()
    for g in range(KV_LOCAL):
        for copy in fetches(g) + loads(g):
            copy.start()
    lane = lax.broadcasted_iota(jnp.int32, (128, 128), 1)
    row = lax.broadcasted_iota(jnp.int32, (128, 128), 0)
    spare = COLS - PARTS * STRIDE
    for g in range(KV_LOCAL):
        at = pl.ds(PARTS * STRIDE, spare)
        keys[g, at, 0:128] = jnp.zeros((spare, 128), jnp.bfloat16)
        keys[g, at, 128:256] = jnp.where(lane == 0, HIDE, 0.0)[:spare].astype(jnp.bfloat16)
        values[g, at, 0:128] = jnp.zeros((spare, 128), jnp.bfloat16)
        values[g, :, 128:256] = jnp.ones((COLS, 128), jnp.bfloat16)
    slot = lane - 64
    part, inner = slot // SPAN, slot % SPAN
    shard = ((info[1] + step_of(part)) % X) * MEMBERS + info[2] * NEAR + info[3]
    token = (info[1] * MEMBERS + place_of(row, info[2], info[3])) * TOK + row % TOK
    hidden = (inner >= TOK) | (shard * TOK + inner > token)
    extra = jnp.where(lane == 0, 1.0, jnp.where((slot >= 0) & hidden, HIDE, 0.0))
    seen[...] = extra.astype(jnp.bfloat16)
    for copy in fetches(KV_LOCAL):
        copy.wait()
    limits = visible_rows(info, q_ref[:, WIDTH : WIDTH + 128].astype(jnp.float32))
    lane = lax.broadcasted_iota(jnp.int32, (STRIDE, 128), 1)
    row = lax.broadcasted_iota(jnp.int32, (STRIDE, 128), 0)
    for k in range(PARTS):
        cached = (lane == 0) & (row < ROWS) & (row.astype(jnp.float32) >= limits[k])
        mark = (row >= ROWS) & (lane == 64 + k * SPAN + row - ROWS)
        bias = jnp.where(cached, HIDE, jnp.where(mark, 1.0, 0.0)).astype(jnp.bfloat16)
        for g in range(KV_LOCAL):
            keys[g, pl.ds(k * STRIDE, STRIDE), 128:256] = bias

    order = places(info[2], info[3])

    def arrange(ref, at, block):
        for piece, place in enumerate(order):
            to = pl.ds(pl.multiple_of(place * TOK, TOK), TOK)
            ref[to, at] = block[piece * TOK : (piece + 1) * TOK]

    per = 2
    lane = lax.broadcasted_iota(jnp.int32, (GTOK, 128), 1)
    mask = jnp.concatenate([seen[...]] * per, axis=0)
    stats = jnp.zeros((GTOK, 128), jnp.float32)
    for g in range(KV_LOCAL):
        for copy in fetches(g) + loads(g):
            copy.wait()

        def columns(h):
            return pl.ds((g * GROUP + h) * 128, 128)

        def score(i):
            heads = [q_ref[:, columns(i * per + j)] for j in range(per)]
            query = jnp.concatenate([jnp.concatenate(heads, axis=0), mask], axis=1)
            return lax.dot_general(
                query, keys[g], (((1,), (1,)), ((), ())), preferred_element_type=jnp.float32
            )

        scores = score(0)
        for i in range(GROUP // per):
            later = score(i + 1) if i + 1 < GROUP // per else None
            top = jnp.max(scores, axis=1, keepdims=True)
            weights = jnp.exp2((scores - top) * (SCALE * LOG2E)).astype(jnp.bfloat16)
            both = jnp.dot(weights, values[g], preferred_element_type=jnp.float32)
            total = both[:, 128:256]
            outs = both[:, 0:128] / total
            lse = top * SCALE + jnp.log(total)
            for j in range(per):
                h = i * per + j
                arrange(res_ref, columns(h), outs[j * GTOK : (j + 1) * GTOK])
                mine = lane % HEADS_LOCAL == g * GROUP + h
                stats = jnp.where(mine, lse[j * GTOK : (j + 1) * GTOK], stats)
            scores = later
        out_ref[:, spans[g]] = res_ref[:, spans[g]].astype(jnp.bfloat16)
        store(g).start()
    arrange(stat_ref, pl.ds(0, 128), stats)
    stats = stat_ref[...]
    high = stats.astype(jnp.bfloat16).astype(jnp.float32)
    rest = stats - high
    middle = rest.astype(jnp.bfloat16).astype(jnp.float32)
    low = rest - middle
    pieces = jnp.where(lane < HEADS_LOCAL, high, jnp.where(lane < 2 * HEADS_LOCAL, middle, low))
    out_ref[:, WIDTH : WIDTH + 128] = pieces.astype(jnp.bfloat16)
    store(KV_LOCAL).start()
    for i in range(KV_LOCAL + 1):
        store(i).wait()


def attend(info, queries, parts):
    hbm = pl.BlockSpec(memory_space=pltpu.HBM)
    operands = [pltpu.with_memory_space_constraint(v, pltpu.HBM) for v in (*queries, *parts)]
    return pl.pallas_call(
        attend_kernel,
        out_shape=pltpu.HBM((GTOK, WIDTH + 128), jnp.bfloat16),
        in_specs=[pl.BlockSpec(memory_space=pltpu.SMEM)] + [hbm] * len(operands),
        out_specs=hbm,
        scratch_shapes=[
            pltpu.VMEM((KV_LOCAL, COLS, 256), jnp.bfloat16),
            pltpu.VMEM((KV_LOCAL, COLS, 256), jnp.bfloat16),
            pltpu.VMEM((GTOK, 128), jnp.bfloat16),
            pltpu.VMEM((GTOK, WIDTH + 128), jnp.bfloat16),
            pltpu.VMEM((GTOK, WIDTH), jnp.float32),
            pltpu.VMEM((GTOK, 128), jnp.float32),
            pltpu.VMEM((GTOK, WIDTH + 128), jnp.bfloat16),
            pltpu.SemaphoreType.DMA((2 * KV_LOCAL * PARTS,)),
            pltpu.SemaphoreType.DMA(((KV_LOCAL + 1) * NEAR,)),
            pltpu.SemaphoreType.DMA((KV_LOCAL + 1,)),
        ],
        compiler_params=pltpu.CompilerParams(vmem_limit_bytes=24 << 20),
        cost_estimate=pl.CostEstimate(
            flops=8 * HEADS_LOCAL * GTOK * COLS * 128,
            bytes_accessed=4 << 20,
            transcendentals=HEADS_LOCAL * GTOK * COLS,
        ),
        name="attend",
    )(info, *operands)


def merge_kernel(got, out_ref):
    pieces = got[:, :, WIDTH : WIDTH + 128].astype(jnp.float32)
    lse = pieces + (pltpu.roll(pieces, 96, 2) + pltpu.roll(pieces, 64, 2))
    share = jnp.exp(lse - jnp.max(lse, axis=0, keepdims=True))
    share = share / jnp.sum(share, axis=0, keepdims=True)
    for h in range(HEADS_LOCAL):
        at = slice(h * 128, (h + 1) * 128)
        merged = jnp.sum(share[:, :, h : h + 1] * got[:, :, at].astype(jnp.float32), axis=0)
        out_ref[:, at] = merged.astype(jnp.bfloat16)


def merge(got):
    vmem = pl.BlockSpec(memory_space=pltpu.VMEM)
    return pl.pallas_call(
        merge_kernel,
        out_shape=jax.ShapeDtypeStruct((TOK, WIDTH), jnp.bfloat16),
        in_specs=[vmem],
        out_specs=vmem,
        compiler_params=pltpu.CompilerParams(vmem_limit_bytes=6 << 20),
        cost_estimate=pl.CostEstimate(flops=2 << 20, bytes_accessed=1 << 20, transcendentals=4096),
        name="merge",
    )(got)


def project_kernel(info, *refs):
    gathered, pieces, (out_ref, rows_ref) = refs[:NEAR], iter(refs[NEAR:-2]), refs[-2:]
    order = places(info[2], info[3])
    merged = jnp.concatenate([ref[...] for ref in gathered], axis=0)
    for k in range(X):
        total, at = None, 0
        while at < WIDTH:
            w = next(pieces)
            rows = w.shape[0]
            term = jnp.dot(merged[:, at : at + rows], w[...], preferred_element_type=jnp.float32)
            total = term if total is None else total + term
            at += rows
        for piece, place in enumerate(order):
            to = pl.ds(pl.multiple_of(place * TOK, TOK), TOK)
            rows_ref[k, to, :] = total[piece * TOK : (piece + 1) * TOK]
        out_ref[(k + info[0] - info[1] + X) % X] = rows_ref[k].astype(jnp.bfloat16)


def project(info, gathered, weights):
    vmem = pl.BlockSpec(memory_space=pltpu.VMEM)
    operands = list(gathered) + [w for part in weights for w in part]
    return pl.pallas_call(
        project_kernel,
        out_shape=jax.ShapeDtypeStruct((X, GTOK, 256), jnp.bfloat16),
        in_specs=[pl.BlockSpec(memory_space=pltpu.SMEM)] + [vmem] * len(operands),
        out_specs=vmem,
        scratch_shapes=[pltpu.VMEM((X, GTOK, 256), jnp.float32)],
        compiler_params=pltpu.CompilerParams(vmem_limit_bytes=14 << 20),
        cost_estimate=pl.CostEstimate(
            flops=2 * GTOK * WIDTH * 256 * X, bytes_accessed=10 << 20, transcendentals=0
        ),
        name="project",
    )(info, *operands)


def along(v, axis, k):
    return lax.ppermute(v, axis, [((i + k) % 4, i) for i in range(4)])


def gather(v):
    some = jnp.concatenate([v] + [along(v, "zq", b) for b in range(1, ZQ)], axis=0)
    return [some] + [along(some, NEAR_AXES, c) for c in range(1, NEAR)]


def after(v, *earlier):
    return lax.optimization_barrier((v, *earlier))[0]


def shards(queries, span_keys, span_values, cache_keys, cache_values, lengths, start_pos, w_out):
    x, zq, near = lax.axis_index("x"), lax.axis_index("zq"), lax.axis_index(NEAR_AXES)
    tp = lax.axis_index(TP_AXES)
    info = jnp.stack([start_pos[0], x, zq, near]).astype(jnp.int32)

    own = collect(cache_keys, cache_values, span_keys, span_values)
    following, previous = along(own, "x", 1), along(own, "x", 3)
    far0 = along(following[: ROWS + SPAN], "x", 1)
    far1 = along(previous[ROWS + SPAN :], "x", 3)

    sizes = [lengths] + [along(lengths, "x", k) for k in STEPS[1:]]
    asked = gather(pack(queries, sizes))

    partial = attend(info, asked, [own, following, previous, far0, far1])
    got = lax.all_to_all(partial.reshape(MEMBERS, TOK, WIDTH + 128), ZY_AXES, 0, 0, tiled=True)

    half = WIDTH // 2
    own_a, own_b = w_out[:half], w_out[half:]
    next_a = along(after(own_a, far0, far1), "x", 1)
    last_b = along(after(own_b, far0, far1), "x", 3)
    far_a = along(after(next_a, last_b), "x", 1)
    far_b = along(after(last_b, next_a), "x", 3)
    next_b = along(after(own_b, far_a, far_b), "x", 1)
    last_a = along(after(own_a, far_a, far_b), "x", 3)
    weights = [(own_a, own_b), (next_a, next_b), (far_a, far_b), (last_a, last_b)]

    attention = gather(after(merge(got), far_a, far_b))

    info = jnp.stack([x, tp, zq, near]).astype(jnp.int32)
    projected = project(info, attention, weights)
    total = None
    for r in range(X):
        pairs = [(a * 4 + b, ((b + r) % X) * 4 + a) for a in range(X) for b in range(4)]
        term = lax.ppermute(projected[r], ("x", "yh", "c"), pairs).astype(jnp.float32)
        total = term if total is None else total + term
    return total.astype(jnp.bfloat16)


def solution(mesh):
    fine = Mesh(mesh.devices.reshape(X, ZQ, ZP, YL, YH, CORE), CTX_AXES + TP_AXES)
    split = P(CTX_AXES, TP_AXES)
    return jax.shard_map(
        shards,
        mesh=fine,
        in_specs=(split, split, split, split, split, P(CTX_AXES), P(), P(TP_AXES, CTX_AXES)),
        out_specs=P(TP_AXES, CTX_AXES),
        check_vma=False,
    )
```

```python
import math

import jax
import jax.numpy as jnp
from jax import lax
from jax.experimental import pallas as pl
from jax.experimental.pallas import tpu as pltpu
from jax.sharding import Mesh, PartitionSpec as P

HEADS = 128
KV_HEADS = 8
HEAD_DIM = 128
GROUP = HEADS // KV_HEADS
HIDE = -1e30
SCALE = 1.0 / math.sqrt(HEAD_DIM)
LOG2E = 1.4426950408889634

X, ZQ, ZP, YL, YH, CORE = 4, 4, 2, 2, 2, 2
NEAR = ZP * YL
MEMBERS = ZQ * NEAR
CTX_AXES = ("x", "zq", "zp", "yl")
TP_AXES = ("yh", "c")
NEAR_AXES = ("zp", "yl")
TOK = 8
ROWS = 512
SPAN = 16
GTOK = MEMBERS * TOK
GATHERED = ZQ * TOK
KV_LOCAL = 2
HEADS_LOCAL = KV_LOCAL * GROUP
WIDTH = HEADS_LOCAL * HEAD_DIM
PARTS = X
STRIDE = ROWS + SPAN
COLS = 2176
STEPS = (0, 1, 3, 2)


def step_of(k):
    return jnp.where(k == 2, 3, jnp.where(k == 3, 2, k))


def collect_kernel(cache_k, cache_v, span_k, span_v, *refs):
    owns, sems = refs[:KV_LOCAL], refs[KV_LOCAL]
    copies = []
    for side, cache in enumerate((cache_k, cache_v)):
        for g in range(KV_LOCAL):
            copies.append(
                pltpu.make_async_copy(
                    cache.at[:, pl.ds(g * 128, 128)],
                    owns[g].at[pl.ds(0, ROWS), pl.ds(side * 128, 128)],
                    sems.at[side * KV_LOCAL + g],
                )
            )
    for copy in copies:
        copy.start()
    empty = jnp.zeros((TOK, 256), jnp.float32)
    for side, span in enumerate((span_k, span_v)):
        padded = jnp.concatenate([span[...].astype(jnp.float32), empty], axis=0)
        padded = padded.astype(jnp.bfloat16)
        for g in range(KV_LOCAL):
            to = slice(side * 128, side * 128 + 128)
            owns[g][ROWS : ROWS + SPAN, to] = padded[:, g * 128 : g * 128 + 128]
    for copy in copies:
        copy.wait()


def collect(cache_keys, cache_values, span_keys, span_values):
    vmem, hbm = pl.BlockSpec(memory_space=pltpu.VMEM), pl.BlockSpec(memory_space=pltpu.HBM)
    caches = [pltpu.with_memory_space_constraint(v, pltpu.HBM) for v in (cache_keys, cache_values)]
    out = jax.ShapeDtypeStruct((STRIDE, 256), jnp.bfloat16)
    return pl.pallas_call(
        collect_kernel,
        out_shape=(out,) * KV_LOCAL,
        in_specs=[hbm, hbm, vmem, vmem],
        out_specs=(vmem,) * KV_LOCAL,
        scratch_shapes=[pltpu.SemaphoreType.DMA((2 * KV_LOCAL,))],
        compiler_params=pltpu.CompilerParams(vmem_limit_bytes=4 << 20),
        cost_estimate=pl.CostEstimate(flops=1 << 16, bytes_accessed=1 << 20, transcendentals=0),
        name="collect",
    )(*caches, span_keys, span_values)


def pack_kernel(queries, size0, size1, size2, size3, message):
    lane = lax.broadcasted_iota(jnp.int32, (TOK, 128), 1)
    tail = jnp.zeros((TOK, 128), jnp.int32)
    for k, size in enumerate((size0, size1, size2, size3)):
        high = size[0] // 256
        tail = jnp.where(lane == k, high, tail)
        tail = jnp.where(lane == PARTS + k, size[0] - high * 256, tail)
    message[:, 0:WIDTH] = queries[...]
    message[:, WIDTH : WIDTH + 128] = tail.astype(jnp.float32).astype(jnp.bfloat16)


def pack(queries, sizes):
    vmem = pl.BlockSpec(memory_space=pltpu.VMEM)
    return pl.pallas_call(
        pack_kernel,
        out_shape=jax.ShapeDtypeStruct((TOK, WIDTH + 128), jnp.bfloat16),
        in_specs=[vmem] + [pl.BlockSpec(memory_space=pltpu.SMEM)] * PARTS,
        out_specs=vmem,
        compiler_params=pltpu.CompilerParams(vmem_limit_bytes=2 << 20),
        cost_estimate=pl.CostEstimate(flops=1 << 16, bytes_accessed=1 << 17, transcendentals=0),
        name="pack",
    )(queries, *sizes)


def places(zq, near):
    return [((zq + b) % ZQ) * NEAR + (near + c) % NEAR for c in range(NEAR) for b in range(ZQ)]


def place_of(rows, zq, near):
    return ((zq + (rows // TOK) % ZQ) % ZQ) * NEAR + (near + rows // GATHERED) % NEAR


def visible_rows(info, tail):
    lane = lax.broadcasted_iota(jnp.int32, (GTOK, 128), 1)
    row = lax.broadcasted_iota(jnp.int32, (GTOK, 128), 0)
    held = (row % TOK == 0) & (lane < 2 * PARTS)
    size = jnp.where(held, tail * jnp.where(lane < PARTS, 256.0, 1.0), 0.0)
    x = (info[1] + step_of(lane % PARTS)) % X
    shard = x * MEMBERS + place_of(row, info[2], info[3])
    start = info[0].astype(jnp.float32)
    out = []
    for k in range(PARTS):
        own = ((info[1] + STEPS[k]) % X) * MEMBERS + info[2] * NEAR + info[3]
        offset = jnp.sum(jnp.where(shard < own, size, 0.0), keepdims=True)
        filled = jnp.sum(jnp.where(shard == own, size, 0.0), keepdims=True)
        out.append(jnp.clip(start - offset, 0.0, filled))
    return out


def in_pieces(values):
    lane = lax.broadcasted_iota(jnp.int32, values.shape, 1)
    high = values.astype(jnp.bfloat16).astype(jnp.float32)
    rest = values - high
    middle = rest.astype(jnp.bfloat16).astype(jnp.float32)
    low = rest - middle
    pieces = jnp.where(lane < HEADS_LOCAL, high, jnp.where(lane < 2 * HEADS_LOCAL, middle, low))
    return pieces.astype(jnp.bfloat16)


def from_pieces(pieces):
    pieces = pieces.astype(jnp.float32)
    return pieces + (pltpu.roll(pieces, 96, 1) + pltpu.roll(pieces, 64, 1))


def attend_kernel(info, *refs):
    q_hbm, parts, rest = refs[:NEAR], refs[NEAR : NEAR + 2 * PARTS], refs[NEAR + 2 * PARTS :]
    outs_hbm, rest = rest[:NEAR], rest[NEAR:]
    keys, values, seen, q_ref, out_ref, kv_sems, q_sems, out_sems = rest
    half = WIDTH // KV_LOCAL
    spans = [pl.ds(g * half, half) for g in range(KV_LOCAL)] + [pl.ds(WIDTH, 128)]

    def fetches(i):
        return [
            pltpu.make_async_copy(
                q_hbm[c].at[:, spans[i]],
                q_ref.at[pl.ds(c * GATHERED, GATHERED), spans[i]],
                q_sems.at[i * NEAR + c],
            )
            for c in range(NEAR)
        ]

    def loads(g):
        copies = []
        for k, kv in enumerate(parts[g * PARTS : (g + 1) * PARTS]):
            for side, to in enumerate((keys, values)):
                copies.append(
                    pltpu.make_async_copy(
                        kv.at[:, pl.ds(side * 128, 128)],
                        to.at[g, pl.ds(k * STRIDE, STRIDE), pl.ds(0, 128)],
                        kv_sems.at[(g * PARTS + k) * 2 + side],
                    )
                )
        return copies

    def stores(i):
        return [
            pltpu.make_async_copy(
                out_ref.at[pl.ds(c * GATHERED, GATHERED), spans[i]],
                outs_hbm[c].at[:, spans[i]],
                out_sems.at[i * NEAR + c],
            )
            for c in range(NEAR)
        ]

    for copy in fetches(KV_LOCAL):
        copy.start()
    for g in range(KV_LOCAL):
        for copy in fetches(g) + loads(g):
            copy.start()
    lane = lax.broadcasted_iota(jnp.int32, (128, 128), 1)
    row = lax.broadcasted_iota(jnp.int32, (128, 128), 0)
    spare = COLS - PARTS * STRIDE
    for g in range(KV_LOCAL):
        at = pl.ds(PARTS * STRIDE, spare)
        keys[g, at, 0:128] = jnp.zeros((spare, 128), jnp.bfloat16)
        keys[g, at, 128:256] = jnp.where(lane == 0, HIDE, 0.0)[:spare].astype(jnp.bfloat16)
        values[g, at, 0:128] = jnp.zeros((spare, 128), jnp.bfloat16)
        values[g, :, 128:256] = jnp.ones((COLS, 128), jnp.bfloat16)
    slot = lane - 64
    part, inner = slot // SPAN, slot % SPAN
    shard = ((info[1] + step_of(part)) % X) * MEMBERS + info[2] * NEAR + info[3]
    token = (info[1] * MEMBERS + place_of(row, info[2], info[3])) * TOK + row % TOK
    hidden = (inner >= TOK) | (shard * TOK + inner > token)
    extra = jnp.where(lane == 0, 1.0, jnp.where((slot >= 0) & hidden, HIDE, 0.0))
    seen[...] = extra.astype(jnp.bfloat16)
    for copy in fetches(KV_LOCAL):
        copy.wait()
    limits = visible_rows(info, q_ref[:, WIDTH : WIDTH + 128].astype(jnp.float32))
    lane = lax.broadcasted_iota(jnp.int32, (STRIDE, 128), 1)
    row = lax.broadcasted_iota(jnp.int32, (STRIDE, 128), 0)
    for k in range(PARTS):
        cached = (lane == 0) & (row < ROWS) & (row.astype(jnp.float32) >= limits[k])
        mark = (row >= ROWS) & (lane == 64 + k * SPAN + row - ROWS)
        bias = jnp.where(cached, HIDE, jnp.where(mark, 1.0, 0.0)).astype(jnp.bfloat16)
        for g in range(KV_LOCAL):
            keys[g, pl.ds(k * STRIDE, STRIDE), 128:256] = bias

    per = 2
    lane = lax.broadcasted_iota(jnp.int32, (GTOK, 128), 1)
    mask = jnp.concatenate([seen[...]] * per, axis=0)
    stats = jnp.zeros((GTOK, 128), jnp.float32)
    for g in range(KV_LOCAL):
        for copy in fetches(g) + loads(g):
            copy.wait()

        def columns(h):
            return pl.ds((g * GROUP + h) * 128, 128)

        def score(i):
            heads = [q_ref[:, columns(i * per + j)] for j in range(per)]
            query = jnp.concatenate([jnp.concatenate(heads, axis=0), mask], axis=1)
            return lax.dot_general(
                query, keys[g], (((1,), (1,)), ((), ())), preferred_element_type=jnp.float32
            )

        scores = score(0)
        for i in range(GROUP // per):
            later = score(i + 1) if i + 1 < GROUP // per else None
            top = jnp.max(scores, axis=1, keepdims=True)
            weights = jnp.exp2((scores - top) * (SCALE * LOG2E)).astype(jnp.bfloat16)
            both = jnp.dot(weights, values[g], preferred_element_type=jnp.float32)
            total = both[:, 128:256]
            outs = (both[:, 0:128] / total).astype(jnp.bfloat16)
            lse = top * SCALE + jnp.log(total)
            for j in range(per):
                h = i * per + j
                out_ref[:, columns(h)] = outs[j * GTOK : (j + 1) * GTOK]
                mine = lane % HEADS_LOCAL == g * GROUP + h
                stats = jnp.where(mine, lse[j * GTOK : (j + 1) * GTOK], stats)
            scores = later
        for copy in stores(g):
            copy.start()
    out_ref[:, WIDTH : WIDTH + 128] = in_pieces(stats)
    for copy in stores(KV_LOCAL):
        copy.start()
    for i in range(KV_LOCAL + 1):
        for copy in stores(i):
            copy.wait()


def attend(info, queries, parts):
    hbm = pl.BlockSpec(memory_space=pltpu.HBM)
    operands = [pltpu.with_memory_space_constraint(v, pltpu.HBM) for v in (*queries, *parts)]
    own = jax.ShapeDtypeStruct((GATHERED, WIDTH + 128), jnp.bfloat16)
    return pl.pallas_call(
        attend_kernel,
        out_shape=(own, *(pltpu.HBM(own.shape, own.dtype),) * (NEAR - 1)),
        in_specs=[pl.BlockSpec(memory_space=pltpu.SMEM)] + [hbm] * len(operands),
        out_specs=(pl.BlockSpec(memory_space=pltpu.VMEM), *(hbm,) * (NEAR - 1)),
        scratch_shapes=[
            pltpu.VMEM((KV_LOCAL, COLS, 256), jnp.bfloat16),
            pltpu.VMEM((KV_LOCAL, COLS, 256), jnp.bfloat16),
            pltpu.VMEM((GTOK, 128), jnp.bfloat16),
            pltpu.VMEM((GTOK, WIDTH + 128), jnp.bfloat16),
            pltpu.VMEM((GTOK, WIDTH + 128), jnp.bfloat16),
            pltpu.SemaphoreType.DMA((2 * KV_LOCAL * PARTS,)),
            pltpu.SemaphoreType.DMA(((KV_LOCAL + 1) * NEAR,)),
            pltpu.SemaphoreType.DMA(((KV_LOCAL + 1) * NEAR,)),
        ],
        compiler_params=pltpu.CompilerParams(vmem_limit_bytes=20 << 20),
        cost_estimate=pl.CostEstimate(
            flops=8 * HEADS_LOCAL * GTOK * COLS * 128,
            bytes_accessed=4 << 20,
            transcendentals=HEADS_LOCAL * GTOK * COLS,
        ),
        name="attend",
    )(info, *operands)


def merge_kernel(*refs):
    gots, outs = refs[:4], refs[4:]
    logs = [from_pieces(got[:, WIDTH : WIDTH + 128]) for got in gots]
    top = jnp.maximum(jnp.maximum(logs[0], logs[1]), jnp.maximum(logs[2], logs[3]))
    shares = [jnp.exp(log - top) for log in logs]
    total = shares[0] + shares[1] + shares[2] + shares[3]
    shares = [share / total for share in shares]
    for h in range(HEADS_LOCAL):
        at = slice(h * 128, (h + 1) * 128)
        merged = sum(
            share[:, h : h + 1] * got[:, at].astype(jnp.float32) for share, got in zip(shares, gots)
        )
        for b, out in enumerate(outs):
            out[:, at] = merged[b * TOK : (b + 1) * TOK].astype(jnp.bfloat16)
    if len(outs) > 1:
        joint = top + jnp.log(total)
        lane = lax.broadcasted_iota(jnp.int32, joint.shape, 1)
        joint = jnp.where(lane < HEADS_LOCAL, joint, 0.0)
        joint = joint + (pltpu.roll(joint, HEADS_LOCAL, 1) + pltpu.roll(joint, 2 * HEADS_LOCAL, 1))
        pieces = in_pieces(joint).astype(jnp.float32)
        for b, out in enumerate(outs):
            out[:, WIDTH : WIDTH + 128] = pieces[b * TOK : (b + 1) * TOK].astype(jnp.bfloat16)


def merge(gots, last):
    vmem = pl.BlockSpec(memory_space=pltpu.VMEM)
    out = jax.ShapeDtypeStruct((TOK, WIDTH if last else WIDTH + 128), jnp.bfloat16)
    return pl.pallas_call(
        merge_kernel,
        out_shape=(out,) * (1 if last else ZQ),
        in_specs=[vmem] * 4,
        out_specs=(vmem,) * (1 if last else ZQ),
        compiler_params=pltpu.CompilerParams(vmem_limit_bytes=6 << 20),
        cost_estimate=pl.CostEstimate(flops=1 << 20, bytes_accessed=1 << 20, transcendentals=4096),
        name="merge",
    )(*gots)


def project_kernel(info, *refs):
    gathered, pieces, (out_ref, rows_ref, held, sems) = refs[:NEAR], refs[NEAR:-4], refs[-4:]
    copies, full = [[] for _ in range(X)], 0
    for i, w in enumerate(pieces):
        k, at = divmod(full, WIDTH)
        rows = w.shape[0]
        copies[k].append(pltpu.make_async_copy(w, held.at[k, pl.ds(at, rows)], sems.at[i]))
        full += rows
    for copy in sum(copies, []):
        copy.start()
    order = places(info[3], info[4])
    merged = jnp.concatenate([ref[...] for ref in gathered], axis=0)
    for k in range(X):
        for copy in copies[k]:
            copy.wait()
        total = jnp.dot(merged, held[k], preferred_element_type=jnp.float32)
        for piece, place in enumerate(order):
            to = pl.ds(pl.multiple_of(place * TOK, TOK), TOK)
            rows_ref[k, to, :] = total[piece * TOK : (piece + 1) * TOK]
        owner = (info[0] + k) % X
        slot = (owner + info[2]) % 2 * 2 + (owner // 2 + info[1]) % 2
        out_ref[slot] = rows_ref[k].astype(jnp.bfloat16)


def project(info, gathered, weights):
    vmem, hbm = pl.BlockSpec(memory_space=pltpu.VMEM), pl.BlockSpec(memory_space=pltpu.HBM)
    weights = [pltpu.with_memory_space_constraint(w, pltpu.HBM) for part in weights for w in part]
    return pl.pallas_call(
        project_kernel,
        out_shape=jax.ShapeDtypeStruct((X, GTOK, 256), jnp.bfloat16),
        in_specs=[pl.BlockSpec(memory_space=pltpu.SMEM)] + [vmem] * NEAR + [hbm] * len(weights),
        out_specs=vmem,
        scratch_shapes=[
            pltpu.VMEM((X, GTOK, 256), jnp.float32),
            pltpu.VMEM((X, WIDTH, 256), jnp.bfloat16),
            pltpu.SemaphoreType.DMA((len(weights),)),
        ],
        compiler_params=pltpu.CompilerParams(vmem_limit_bytes=16 << 20),
        cost_estimate=pl.CostEstimate(
            flops=2 * GTOK * WIDTH * 256 * X, bytes_accessed=10 << 20, transcendentals=0
        ),
        name="project",
    )(info, *gathered, *weights)


def along(v, axis, k):
    return lax.ppermute(v, axis, [((i + k) % 4, i) for i in range(4)])


def gather(v, *earlier):
    some = jnp.concatenate([v] + [along(v, "zq", b) for b in range(1, ZQ)], axis=0)
    some = after(some, *earlier) if earlier else some
    return [some] + [along(some, NEAR_AXES, c) for c in range(1, NEAR)]


def after(v, *earlier):
    return lax.optimization_barrier((v, *earlier))[0]


def shards(queries, span_keys, span_values, cache_keys, cache_values, lengths, start_pos, w_out):
    x, zq, near = lax.axis_index("x"), lax.axis_index("zq"), lax.axis_index(NEAR_AXES)
    info = jnp.stack([start_pos[0], x, zq, near]).astype(jnp.int32)

    own = collect(cache_keys, cache_values, span_keys, span_values)
    following, previous = [along(v, "x", 1) for v in own], [along(v, "x", 3) for v in own]
    far = [along(following[0], "x", 1), along(previous[1], "x", 3)]
    parts = [v[g] for g in range(KV_LOCAL) for v in (own, following, previous, far)]

    sizes = [lengths] + [along(lengths, "x", k) for k in STEPS[1:]]
    asked = gather(after(pack(queries, sizes), following[0], previous[0]))

    half, few = WIDTH // 2, 1408
    held = after(w_out, asked[0])
    next_a = along(after(held[:-few], *far), "x", 1)
    last_b = along(after(held[few:], *far), "x", 3)

    partial = attend(info, asked, parts)
    got = [partial[0]] + [along(partial[c], NEAR_AXES, NEAR - c) for c in range(1, NEAR)]
    far_a = along(after(next_a[:half], *got[1:]), "x", 1)
    far_b = along(after(last_b[half - few :], *got[1:]), "x", 3)
    joined = merge(got, False)
    got = [joined[0]] + [along(joined[b], "zq", ZQ - b) for b in range(1, ZQ)]
    next_b = along(after(w_out[-few:], far_a, far_b), "x", 1)
    last_a = along(after(w_out[:few], far_a, far_b), "x", 3)
    weights = [[w_out], [next_a, next_b], [far_a, far_b], [last_a, last_b]]
    attention = gather(merge(got, True)[0], far_a, far_b)

    yh, core = lax.axis_index("yh"), lax.axis_index("c")
    info = jnp.stack([x, yh, core, zq, near]).astype(jnp.int32)
    projected = project(info, attention, weights)
    taken = lax.ppermute(projected[2:], "c", [(0, 1), (1, 0)])
    terms = []
    for r in range(X // 2):
        pair = (projected[r].astype(jnp.float32) + taken[r].astype(jnp.float32)).astype(jnp.bfloat16)
        pairs = [
            ((a * 2 + h) * 2 + c, (c + 2 * ((h + r) % 2)) * 4 + a)
            for a in range(X)
            for h in range(YH)
            for c in range(CORE)
        ]
        terms.append(lax.ppermute(pair, ("x", "yh", "c"), pairs).astype(jnp.float32))
    return (terms[0] + terms[1]).astype(jnp.bfloat16)


def solution(mesh):
    fine = Mesh(mesh.devices.reshape(X, ZQ, ZP, YL, YH, CORE), CTX_AXES + TP_AXES)
    split = P(CTX_AXES, TP_AXES)
    return jax.shard_map(
        shards,
        mesh=fine,
        in_specs=(split, split, split, split, split, P(CTX_AXES), P(), P(TP_AXES, CTX_AXES)),
        out_specs=P(TP_AXES, CTX_AXES),
        check_vma=False,
    )
```
